32 devices in a mesh: src: 8 (over y, x, core), dst: 4 (over z).
Axes of the slice: x: 2, y: 2, z: 4, core: 2. Of those that a mesh axis runs over, the one named last changes fastest.
Arguments:
- src_table: float32 [512, 8, 400], P('dst', 'src'), may hold values from -1.8 to 1.8
- src_state: float32 [512, 8], P('dst', 'src'), may hold values from 0.05 to 2
- dst_table: float32 [1024, 4, 400], P('src', 'dst'), may hold values from -20 to 20
- dst_state: float32 [1024, 4], P('src', 'dst'), may hold values from 0.05 to 2
- rel_table: float32 [16, 400], replicated, may hold values from 0.1 to 1.9
- rel_state: float32 [16], replicated, may hold values from 0.5 to 5
- src_rows: int32 [8, 4, 4096], P('src', 'dst'), may hold values from 0 to 511
- dst_rows: int32 [8, 4, 4096], P('src', 'dst'), may hold values from 0 to 1023
- rel_ids: int32 [8, 4, 4096], P('src', 'dst'), may hold values from 0 to 15
- counts: int32 [8, 4], P('src', 'dst'), may hold values from 256 to 4096, as said below
- neg_rows: int32 [8, 4, 4, 1024], P('src', 'dst'), may hold values from 0 to 1023
Outputs:
- new_src: float32 [512, 8, 400], P('dst', 'src')
- new_src_state: float32 [512, 8], P('dst', 'src')
- new_dst: float32 [1024, 4, 400], P('src', 'dst')
- new_dst_state: float32 [1024, 4], P('src', 'dst')
- new_rel: float32 [16, 400], replicated
- new_rel_state: float32 [16], replicated
The draws below stay inside these ranges and needn't reach their ends.
Inputs may be any that keep to these rules, and one draw needn't show every extreme that they name: One bucket holds at most 4096 edges; only the first counts[i, j] slots of a bucket are real edges.
All inputs are finite; a program needn't handle non-finite values.
Results may differ from the reference program's by a relative error of at most 0.0093.
Values may be sent and summed in bfloat16 or wider, within the bound.
A program may use at most 128 MiB of HBM per device.

```python
import math
import jax
import jax.numpy as jnp
from jax import lax

D = 400
REL = 16
EDGE_CAP = 4096
BLOCK = 1024
NEG = 1024
BLOCKS = 4
SRC_PART = 512
DST_PART = 1024
N_SRC = 8
N_DST = 4


def draw_dst_table(key, part):
    key = jax.random.fold_in(key, 7)
    first = jax.random.fold_in(key, 0)
    shape = (DST_PART, N_DST, D)
    return jnp.clip(0.3 * jax.random.normal(first, shape, jnp.float32), -1.8, 1.8)


def draw_counts(key, part):
    key = jax.random.fold_in(key, 3)
    first, second, third = jax.random.split(key, 3)
    level = jax.random.randint(first, (N_SRC, N_DST), 0, 4)
    ceiling = jnp.right_shift(jnp.int32(EDGE_CAP), level)
    taken = jax.random.randint(second, (N_SRC, N_DST), 0, ceiling // 2 + 1)
    values = (ceiling - taken).reshape(-1)
    chosen = jax.random.randint(third, (), 0, N_SRC * N_DST)
    values = values.at[chosen].set(EDGE_CAP)
    return values.reshape(N_SRC, N_DST).astype(jnp.int32)


def touch_ends(drawn, key, low, top_value):
    place = [jax.random.randint(jax.random.fold_in(key, axis), (), 0, length) for axis, length in enumerate(drawn.shape)]
    widest = drawn.shape.index(max(drawn.shape))
    next_to = place[:widest] + [(place[widest] + 1) % drawn.shape[widest]] + place[widest + 1:]
    return drawn.at[tuple(place)].set(low).at[tuple(next_to)].set(top_value)


def block_levels(key, dims, shards, low, largest):
    gain, own = 1.0, jax.random.fold_in(key, 6)
    for axis_at, blocks in shards:
        draws = jnp.exp(jax.random.uniform(jax.random.fold_in(own, axis_at), (blocks,), jnp.float32, low / len(shards), largest / len(shards)))
        gain = gain * jnp.repeat(draws, dims[axis_at] // blocks).reshape([-1 if axis == axis_at else 1 for axis in range(len(dims))])
    return gain


def bell_draw(rng, dims, scale, reach, cuts=(), kind=jnp.bfloat16):
    array = scale * jax.random.normal(rng, dims, jnp.float32)
    if cuts:
        array = array * block_levels(rng, dims, cuts, -0.22, 0.18)
    return jnp.clip(array, -reach, reach).astype(kind)


def setup_inputs(seed: int = 0) -> dict:
    keys = jax.random.split(jax.random.key(seed), 12)
    return {
        "src_table": bell_draw(keys[0], (SRC_PART, N_SRC, D), 0.3, 1.8, ((0, 4), (1, 8)), jnp.float32),
        "src_state": jnp.clip(jnp.exp(math.log(2.0) - 3.6888794 * jax.random.uniform(keys[1], (SRC_PART, N_SRC), jnp.float32) ** block_levels(keys[1], (SRC_PART, N_SRC), ((0, 4), (1, 8)), -0.2, 0.2)), 0.05, 2.0),
        "dst_table": draw_dst_table(jax.random.fold_in(keys[11], 71), 0),
        "dst_state": jnp.clip(jnp.exp(math.log(2.0) - 3.6888794 * jax.random.uniform(keys[3], (DST_PART, N_DST), jnp.float32) ** block_levels(keys[3], (DST_PART, N_DST), ((0, 8), (1, 4)), -0.2, 0.2)), 0.05, 2.0),
        "rel_table": jnp.clip(1.0 + 0.18 * jax.random.normal(keys[4], (REL, D), jnp.float32), 0.1, 1.9),
        "rel_state": jnp.clip(jnp.exp(jax.random.uniform(keys[5], (REL,), jnp.float32, math.log(0.5), math.log(5.0))), 0.5, 5.0),
        "src_rows": touch_ends(jax.random.randint(keys[6], (N_SRC, N_DST, EDGE_CAP), 0, SRC_PART), jax.random.fold_in(keys[6], 1), 0, SRC_PART - 1).astype(jnp.int32),
        "dst_rows": touch_ends(jax.random.randint(keys[7], (N_SRC, N_DST, EDGE_CAP), 0, DST_PART), jax.random.fold_in(keys[7], 1), 0, DST_PART - 1).astype(jnp.int32),
        "rel_ids": touch_ends(jax.random.randint(keys[8], (N_SRC, N_DST, EDGE_CAP), 0, REL), jax.random.fold_in(keys[8], 1), 0, REL - 1).astype(jnp.int32),
        "counts": draw_counts(jax.random.fold_in(keys[11], 71), 0),
        "neg_rows": touch_ends(jax.random.randint(keys[10], (N_SRC, N_DST, BLOCKS, NEG), 0, DST_PART), jax.random.fold_in(keys[10], 1), 0, DST_PART - 1).astype(jnp.int32),
    }


LEARN_RATE = 0.1

def block_terms(start, width_block, block_index, src_part, dst_part, rel_table, s_all, t_all, r_all, negs, count):
    src_idx = lax.dynamic_slice_in_dim(s_all, start, width_block)
    dst_idx = lax.dynamic_slice_in_dim(t_all, start, width_block)
    rel_idx = lax.dynamic_slice_in_dim(r_all, start, width_block)
    neg_idx = lax.dynamic_index_in_dim(negs, block_index, 0, keepdims=False)
    slots = start + jnp.arange(width_block, dtype=jnp.int32)
    valid = (slots < count).astype(jnp.float32)
    onehot = (rel_idx[:, None] == jnp.arange(rel_table.shape[0], dtype=jnp.int32)[None, :]).astype(jnp.float32)
    rel_rows = jnp.dot(onehot, rel_table, precision=lax.Precision.HIGHEST)
    src_emb = jnp.take(src_part, src_idx, axis=0)
    src_wide = src_emb.astype(jnp.float32)
    query = (src_wide * rel_rows).astype(jnp.bfloat16)
    query_wide = query.astype(jnp.float32)
    dst_emb = jnp.take(dst_part, dst_idx, axis=0)
    dst_wide = dst_emb.astype(jnp.float32)
    neg_emb = jnp.take(dst_part, neg_idx, axis=0)
    pos = lax.optimization_barrier(jnp.sum(query_wide * dst_wide, axis=-1))
    neg = lax.dot_general(query, neg_emb, (((1,), (1,)), ((), ())), preferred_element_type=jnp.float32)
    top = jnp.maximum(pos, lax.optimization_barrier(jnp.max(neg, axis=-1)))
    pos_exp = jnp.exp(pos - top)
    neg_exp = jnp.exp(neg - top[:, None])
    total = pos_exp + lax.optimization_barrier(jnp.sum(neg_exp, axis=-1))
    pos_coef = valid * (pos_exp / total - 1.0)
    neg_weight = (valid[:, None] * neg_exp / total[:, None]).astype(jnp.bfloat16)
    dquery = jnp.dot(neg_weight, neg_emb, preferred_element_type=jnp.float32) + pos_coef[:, None] * dst_wide
    src_term = dquery * rel_rows
    rel_term = lax.dot_general(onehot, dquery * src_wide, (((0,), (0,)), ((), ())), precision=lax.Precision.HIGHEST)
    dst_pos = pos_coef[:, None] * query_wide
    dst_neg = lax.dot_general(neg_weight, query, (((0,), (0,)), ((), ())), preferred_element_type=jnp.float32)
    return (src_idx, src_term, dst_idx, dst_pos, neg_idx, dst_neg, rel_term)

def adagrad(table, state, grad):
    new_state = state + lax.optimization_barrier(jnp.mean(grad * grad, axis=-1))
    return (table - LEARN_RATE * grad / jnp.sqrt(new_state)[..., None], new_state)

def reference(src_table, src_state, dst_table, dst_state, rel_table, rel_state, src_rows, dst_rows, rel_ids, counts, neg_rows):
    src_low = src_table.astype(jnp.bfloat16)
    dst_low = dst_table.astype(jnp.bfloat16)
    width = src_table.shape[-1]

    def bucket(carry, flat):
        src_grad, dst_grad, rel_grad = carry
        row_i = flat // N_DST
        col_j = flat % N_DST
        src_part = lax.dynamic_index_in_dim(src_low, row_i, 1, keepdims=False)
        dst_part = lax.dynamic_index_in_dim(dst_low, col_j, 1, keepdims=False)
        s_all = src_rows[row_i, col_j]
        t_all = dst_rows[row_i, col_j]
        r_all = rel_ids[row_i, col_j]
        negs = neg_rows[row_i, col_j]
        count = counts[row_i, col_j]

        def block_step(inner, block_index):
            part_src, part_dst, part_rel = inner
            got = block_terms(block_index * BLOCK, BLOCK, block_index, src_part, dst_part, rel_table, s_all, t_all, r_all, negs, count)
            src_idx, src_term, dst_idx, dst_pos, neg_idx, dst_neg, rel_term = got
            part_src = part_src.at[src_idx].add(src_term)
            part_dst = part_dst.at[dst_idx].add(dst_pos).at[neg_idx].add(dst_neg)
            return ((part_src, part_dst, part_rel + rel_term), None)
        start = (jnp.zeros((SRC_PART, width), jnp.float32), jnp.zeros((DST_PART, width), jnp.float32), jnp.zeros((REL, width), jnp.float32))
        (part_src, part_dst, part_rel), _ = lax.scan(block_step, start, jnp.arange(BLOCKS, dtype=jnp.int32))
        src_grad = src_grad.at[:, row_i].add(part_src)
        dst_grad = dst_grad.at[:, col_j].add(part_dst)
        return ((src_grad, dst_grad, rel_grad + part_rel), None)
    start = (jnp.zeros(src_table.shape, jnp.float32), jnp.zeros(dst_table.shape, jnp.float32), jnp.zeros(rel_table.shape, jnp.float32))
    (src_grad, dst_grad, rel_grad), _ = lax.scan(bucket, start, jnp.arange(N_SRC * N_DST, dtype=jnp.int32))
    new_src, new_src_state = adagrad(src_table, src_state, src_grad)
    new_dst, new_dst_state = adagrad(dst_table, dst_state, dst_grad)
    new_rel, new_rel_state = adagrad(rel_table, rel_state, rel_grad)
    return (new_src, new_src_state, new_dst, new_dst_state, new_rel, new_rel_state)
```

```python
import functools

import jax
import jax.numpy as jnp
from jax import lax
from jax.experimental import pallas as pl
from jax.experimental.pallas import tpu as pltpu
from jax.sharding import PartitionSpec as P

LEARN_RATE = 0.1
CHUNK = 512
LOWEST = -1e30

NN = (((1,), (0,)), ((), ()))
NT = (((1,), (1,)), ((), ()))


def mm(a, b, dims=NN):
    return lax.dot_general(a, b, dims, preferred_element_type=jnp.float32)


def split(x):
    high = x.astype(jnp.bfloat16)
    return high, (x - high.astype(jnp.float32)).astype(jnp.bfloat16)


def one_hot(rows, idx):
    row = lax.broadcasted_iota(jnp.int32, (rows, idx.shape[1]), 0)
    return (row == idx).astype(jnp.float32).astype(jnp.bfloat16)


def bucket_kernel(
    per_block,
    count_ref,
    s_ref,
    t_ref,
    r_ref,
    neg_ref,
    src_t_ref,
    dst_ref,
    dst_t_ref,
    rel_parts_ref,
    src_grad_ref,
    dst_grad_ref,
    rel_grad_ref,
    times_ref,
):
    src_grad_ref[...] = jnp.zeros_like(src_grad_ref)
    dst_grad_ref[...] = jnp.zeros_like(dst_grad_ref)
    rel_grad_ref[...] = jnp.zeros_like(rel_grad_ref)
    count = count_ref[0]
    chunk = s_ref.shape[2]
    src_rows = src_t_ref.shape[1]
    dst_rows = dst_ref.shape[0]
    relations = rel_grad_ref.shape[1]

    @pl.loop(0, (count + chunk - 1) // chunk)
    def _(step):
        @pl.when(lax.rem(step, per_block) == 0)
        def _():
            neg = neg_ref[lax.div(step, per_block)]
            row = lax.broadcasted_iota(jnp.int32, (dst_rows, neg.shape[1]), 0)
            times = jnp.sum((row == neg).astype(jnp.float32), axis=1, keepdims=True)
            times_ref[...] = jnp.broadcast_to(times, times_ref.shape)

        slots = step * chunk + lax.broadcasted_iota(jnp.int32, (1, chunk), 1)
        valid = (slots < count).astype(jnp.float32)
        src_hot = one_hot(src_rows, s_ref[step])
        rel_hot = one_hot(relations, r_ref[step])
        src_emb = mm(src_t_ref[...], src_hot)
        rel_rows = mm(rel_parts_ref[...], jnp.concatenate([rel_hot] * 3, axis=0))
        query = (src_emb * rel_rows).astype(jnp.bfloat16)
        score = mm(dst_ref[...], query)
        is_pos = lax.broadcasted_iota(jnp.int32, score.shape, 0) == t_ref[step]
        times = times_ref[...]
        times = jnp.where(is_pos, times + 1.0, times)
        score = jnp.where(times > 0.0, score, LOWEST)
        top = jnp.max(score, axis=0, keepdims=True)
        terms = times * jnp.exp(score - top)
        weight = terms * (valid / jnp.sum(terms, axis=0, keepdims=True))
        weight = jnp.where(is_pos, weight - valid, weight)
        high, low = split(weight)
        dst_grad_ref[...] += mm(high, query, NT) + mm(low, query, NT)
        dquery = mm(dst_t_ref[...], high) + mm(dst_t_ref[...], low)
        high, low = split(dquery * rel_rows)
        src_grad_ref[...] += mm(src_hot, high, NT) + mm(src_hot, low, NT)
        high, low = split(dquery * src_emb)
        rel_grad_ref[...] += mm(high, rel_hot, NT) + mm(low, rel_hot, NT)


def bucket_grads(src_part, dst_part, rel_table, s_all, t_all, r_all, negs, count):
    blocks, negatives = negs.shape
    width_block = s_all.shape[0] // blocks
    chunk = CHUNK if width_block % CHUNK == 0 else width_block
    steps = s_all.shape[0] // chunk
    high = lax.reduce_precision(rel_table, 8, 7)
    middle = lax.reduce_precision(rel_table - high, 8, 7)
    rel_parts = jnp.concatenate([high, middle, rel_table - high - middle], axis=0)
    vmem = pl.BlockSpec(memory_space=pltpu.VMEM)
    width = rel_table.shape[1]
    src_sum, dst_sum, rel_sum = pl.pallas_call(
        functools.partial(bucket_kernel, width_block // chunk),
        out_shape=(
            jax.ShapeDtypeStruct(src_part.shape, jnp.float32),
            jax.ShapeDtypeStruct(dst_part.shape, jnp.float32),
            jax.ShapeDtypeStruct((width, rel_table.shape[0]), jnp.float32),
        ),
        in_specs=[pl.BlockSpec(memory_space=pltpu.SMEM)] + [vmem] * 8,
        out_specs=[vmem] * 3,
        scratch_shapes=[pltpu.VMEM((dst_part.shape[0], chunk), jnp.float32)],
        compiler_params=pltpu.CompilerParams(vmem_limit_bytes=56 * 2**20),
    )(
        count.reshape(1),
        s_all.reshape(steps, 1, chunk),
        t_all.reshape(steps, 1, chunk),
        r_all.reshape(steps, 1, chunk),
        negs.reshape(blocks, 1, negatives),
        src_part.T,
        dst_part,
        dst_part.T,
        rel_parts.astype(jnp.bfloat16).T,
    )
    return src_sum, dst_sum, rel_sum.T


def adagrad(table, state, grad):
    new_state = state + jnp.mean(grad * grad, axis=-1)
    return (table - LEARN_RATE * grad / jnp.sqrt(new_state)[..., None], new_state)


def body(
    src_table,
    src_state,
    dst_table,
    dst_state,
    rel_table,
    rel_state,
    src_rows,
    dst_rows,
    rel_ids,
    counts,
    neg_rows,
):
    rows, _, width = src_table.shape
    src_part = lax.all_gather(src_table.astype(jnp.bfloat16), "dst", axis=0, tiled=True).reshape(
        -1, width
    )
    dst_part = lax.all_gather(dst_table.astype(jnp.bfloat16), "src", axis=0, tiled=True).reshape(
        -1, width
    )
    s_all = src_rows.reshape(-1)
    t_all = dst_rows.reshape(-1)
    r_all = rel_ids.reshape(-1)
    negs = neg_rows.reshape(neg_rows.shape[2], neg_rows.shape[3])
    count = counts.reshape(())
    src_sum, dst_sum, rel_sum = bucket_grads(
        src_part, dst_part, rel_table, s_all, t_all, r_all, negs, count
    )
    src_grad = lax.psum_scatter(src_sum, "dst", scatter_dimension=0, tiled=True)
    dst_grad = lax.psum_scatter(dst_sum, "src", scatter_dimension=0, tiled=True)
    rel_grad = lax.psum(rel_sum, ("src", "dst"))
    new_src, new_src_state = adagrad(src_table, src_state, src_grad.reshape(src_table.shape))
    new_dst, new_dst_state = adagrad(dst_table, dst_state, dst_grad.reshape(dst_table.shape))
    new_rel, new_rel_state = adagrad(rel_table, rel_state, rel_grad)
    return (new_src, new_src_state, new_dst, new_dst_state, new_rel, new_rel_state)


def solution(mesh):
    return jax.shard_map(
        body,
        mesh=mesh,
        in_specs=(
            P("dst", "src", None),
            P("dst", "src"),
            P("src", "dst", None),
            P("src", "dst"),
            P(),
            P(),
            P("src", "dst", None),
            P("src", "dst", None),
            P("src", "dst", None),
            P("src", "dst"),
            P("src", "dst", None, None),
        ),
        out_specs=(
            P("dst", "src", None),
            P("dst", "src"),
            P("src", "dst", None),
            P("src", "dst"),
            P(),
            P(),
        ),
        check_vma=False,
    )
```

```python
import functools

import jax
import jax.numpy as jnp
from jax import lax
from jax.experimental import pallas as pl
from jax.experimental.pallas import tpu as pltpu
from jax.sharding import PartitionSpec as P

LEARN_RATE = 0.1
CHUNK = 512
LOWEST = -1e30

NN = (((1,), (0,)), ((), ()))
NT = (((1,), (1,)), ((), ()))


def mm(a, b, dims=NN):
    return lax.dot_general(a, b, dims, preferred_element_type=jnp.float32)


def split(x):
    high = x.astype(jnp.bfloat16)
    return high, (x - high.astype(jnp.float32)).astype(jnp.bfloat16)


def one_hot(rows, idx):
    row = lax.broadcasted_iota(jnp.int32, (rows, idx.shape[1]), 0)
    return (row == idx).astype(jnp.float32).astype(jnp.bfloat16)


def bucket_kernel(
    per_block,
    count_ref,
    s_ref,
    t_ref,
    r_ref,
    neg_ref,
    src_t_ref,
    dst_ref,
    dst_t_ref,
    rel_parts_ref,
    src_grad_ref,
    dst_grad_ref,
    rel_sum_ref,
    rel_grad_ref,
    times_ref,
):
    src_grad_ref[...] = jnp.zeros_like(src_grad_ref)
    dst_grad_ref[...] = jnp.zeros_like(dst_grad_ref)
    rel_grad_ref[...] = jnp.zeros_like(rel_grad_ref)
    count = count_ref[0]
    chunk = s_ref.shape[2]
    src_rows = src_t_ref.shape[1]
    dst_rows = dst_ref.shape[0]
    relations = rel_grad_ref.shape[1]

    @pl.loop(0, (count + chunk - 1) // chunk)
    def _(step):
        @pl.when(lax.rem(step, per_block) == 0)
        def _():
            neg = neg_ref[lax.div(step, per_block)]
            row = lax.broadcasted_iota(jnp.int32, (dst_rows, neg.shape[1]), 0)
            times = jnp.sum((row == neg).astype(jnp.float32), axis=1, keepdims=True)
            times_ref[...] = jnp.broadcast_to(times, times_ref.shape)

        slots = step * chunk + lax.broadcasted_iota(jnp.int32, (1, chunk), 1)
        valid = (slots < count).astype(jnp.float32)
        src_hot = one_hot(src_rows, s_ref[step])
        rel_hot = one_hot(relations, r_ref[step])
        src_emb = mm(src_t_ref[...], src_hot)
        rel_rows = mm(rel_parts_ref[...], jnp.concatenate([rel_hot] * 3, axis=0))
        query = (src_emb * rel_rows).astype(jnp.bfloat16)
        score = mm(dst_ref[...], query)
        is_pos = lax.broadcasted_iota(jnp.int32, score.shape, 0) == t_ref[step]
        times = times_ref[...]
        times = jnp.where(is_pos, times + 1.0, times)
        score = jnp.where(times > 0.0, score, LOWEST)
        top = jnp.max(score, axis=0, keepdims=True)
        terms = times * jnp.exp(score - top)
        weight = terms * (valid / jnp.sum(terms, axis=0, keepdims=True))
        weight = jnp.where(is_pos, weight - valid, weight)
        high, low = split(weight)
        dst_grad_ref[...] += mm(query, high, NT) + mm(query, low, NT)
        dquery = mm(dst_t_ref[...], high) + mm(dst_t_ref[...], low)
        high, low = split(dquery * rel_rows)
        src_grad_ref[...] += mm(high, src_hot, NT) + mm(low, src_hot, NT)
        high, low = split(dquery * src_emb)
        rel_grad_ref[...] += mm(high, rel_hot, NT) + mm(low, rel_hot, NT)

    row = lax.broadcasted_iota(jnp.int32, (relations, relations), 0)
    column = lax.broadcasted_iota(jnp.int32, (relations, relations), 1)
    rel_sum_ref[...] = lax.dot_general(
        (row == column).astype(jnp.float32),
        rel_grad_ref[...],
        NT,
        precision=lax.Precision.HIGHEST,
        preferred_element_type=jnp.float32,
    )


def exchange(axis, n, pairs, send_sem, recv_sem):
    me = lax.axis_index(axis)
    copies = []
    for k in range(1, n):
        peer = lax.rem(me + k, n)
        source, target = pairs(me, peer)
        copies.append(
            pltpu.make_async_remote_copy(
                src_ref=source,
                dst_ref=target,
                send_sem=send_sem.at[k - 1],
                recv_sem=recv_sem.at[k - 1],
                device_id={axis: peer},
                device_id_type=pl.DeviceIdType.MESH,
            )
        )
    for copy in copies:
        copy.start()
    return copies


def greet(sizes):
    barrier = pltpu.get_barrier_semaphore()
    for axis, n in sizes:
        me = lax.axis_index(axis)
        for k in range(1, n):
            pl.semaphore_signal(
                barrier,
                inc=1,
                device_id={axis: lax.rem(me + k, n)},
                device_id_type=pl.DeviceIdType.MESH,
            )
    pl.semaphore_wait(barrier, sum(n - 1 for _, n in sizes))


def lanes(index, rows):
    return pl.ds(pl.multiple_of(index * rows, rows), rows)


def gather_kernel(n_src, n_dst, src_ref, dst_ref, src_all, dst_all, sends, recvs, send2, recv2):
    greet((("src", n_src), ("dst", n_dst)))
    rows = dst_ref.shape[1]
    mine = lanes(lax.axis_index("src"), rows)
    copies = exchange(
        "src", n_src, lambda me, peer: (dst_ref, dst_all.at[:, lanes(me, rows)]), sends, recvs
    )
    own_rows = src_ref.shape[1]
    own = lanes(lax.axis_index("dst"), own_rows)
    copies += exchange(
        "dst", n_dst, lambda me, peer: (src_ref, src_all.at[:, lanes(me, own_rows)]), send2, recv2
    )
    dst_all[:, mine] = dst_ref[...]
    src_all[:, own] = src_ref[...]
    for copy in copies:
        copy.wait()


def gather(src_low, dst_low, n_src, n_dst):
    vmem = pl.BlockSpec(memory_space=pltpu.VMEM)
    dma = pltpu.SemaphoreType.DMA
    width = src_low.shape[0]
    return pl.pallas_call(
        functools.partial(gather_kernel, n_src, n_dst),
        out_shape=(
            jax.ShapeDtypeStruct((width, src_low.shape[1] * n_dst), jnp.bfloat16),
            jax.ShapeDtypeStruct((width, dst_low.shape[1] * n_src), jnp.bfloat16),
        ),
        in_specs=[vmem] * 2,
        out_specs=[vmem] * 2,
        scratch_shapes=[
            dma((n_src - 1,)),
            dma((n_src - 1,)),
            dma((n_dst - 1,)),
            dma((n_dst - 1,)),
        ],
        compiler_params=pltpu.CompilerParams(
            collective_id=0, has_side_effects=True, vmem_limit_bytes=32 * 2**20
        ),
    )(src_low, dst_low)


def total(slots, n):
    value = slots[0]
    for k in range(1, n):
        value = value + slots[k]
    return value


def reduce_kernel(
    n_src,
    n_dst,
    src_ref,
    dst_ref,
    rel_ref,
    src_out,
    dst_out,
    rel_out,
    src_slots,
    dst_slots,
    rel_slots,
    rel_slots2,
    part,
    *sems,
):
    greet((("src", n_src), ("dst", n_dst)))
    i, j = lax.axis_index("src"), lax.axis_index("dst")
    dst_rows, src_rows = dst_out.shape[1], src_out.shape[1]
    first = exchange("src", n_src, lambda me, peer: (rel_ref, rel_slots.at[me]), *sems[0:2])
    copies = exchange(
        "src",
        n_src,
        lambda me, peer: (dst_ref.at[:, lanes(peer, dst_rows)], dst_slots.at[me]),
        *sems[2:4],
    )
    src_copies = exchange(
        "dst",
        n_dst,
        lambda me, peer: (src_ref.at[:, lanes(peer, src_rows)], src_slots.at[me]),
        *sems[4:6],
    )
    rel_slots[i] = rel_ref[...]
    dst_slots[i] = dst_ref[:, lanes(i, dst_rows)]
    src_slots[j] = src_ref[:, lanes(j, src_rows)]
    for copy in first:
        copy.wait()
    part[...] = total(rel_slots, n_src)
    rel_slots2[j] = part[...]
    second = exchange("dst", n_dst, lambda me, peer: (part, rel_slots2.at[me]), *sems[6:8])
    for copy in src_copies:
        copy.wait()
    src_out[...] = total(src_slots, n_dst)
    for copy in second:
        copy.wait()
    rel_out[...] = total(rel_slots2, n_dst)
    for copy in copies:
        copy.wait()
    dst_out[...] = total(dst_slots, n_src)


def reduce(src_sum, dst_sum, rel_sum, n_src, n_dst):
    vmem = pl.BlockSpec(memory_space=pltpu.VMEM)
    dma = pltpu.SemaphoreType.DMA
    width = src_sum.shape[0]
    src_piece = (width, src_sum.shape[1] // n_dst)
    dst_piece = (width, dst_sum.shape[1] // n_src)
    counts = (n_src, n_src, n_dst, n_dst)
    return pl.pallas_call(
        functools.partial(reduce_kernel, n_src, n_dst),
        out_shape=tuple(
            jax.ShapeDtypeStruct(shape, jnp.float32)
            for shape in (src_piece, dst_piece, rel_sum.shape)
        ),
        in_specs=[vmem] * 3,
        out_specs=[vmem] * 3,
        scratch_shapes=[
            pltpu.VMEM((n_dst,) + src_piece, jnp.float32),
            pltpu.VMEM((n_src,) + dst_piece, jnp.float32),
            pltpu.VMEM((n_src,) + rel_sum.shape, jnp.float32),
            pltpu.VMEM((n_dst,) + rel_sum.shape, jnp.float32),
            pltpu.VMEM(rel_sum.shape, jnp.float32),
        ]
        + [dma((n - 1,)) for n in counts for _ in range(2)],
        compiler_params=pltpu.CompilerParams(
            collective_id=1, has_side_effects=True, vmem_limit_bytes=48 * 2**20
        ),
    )(src_sum, dst_sum, rel_sum)


def bucket_grads(src_t, dst_t, rel_table, s_all, t_all, r_all, negs, count):
    blocks, negatives = negs.shape
    width_block = s_all.shape[0] // blocks
    chunk = CHUNK if width_block % CHUNK == 0 else width_block
    steps = s_all.shape[0] // chunk
    high = lax.reduce_precision(rel_table, 8, 7)
    middle = lax.reduce_precision(rel_table - high, 8, 7)
    rel_parts = jnp.concatenate([high, middle, rel_table - high - middle], axis=0)
    vmem = pl.BlockSpec(memory_space=pltpu.VMEM)
    width = rel_table.shape[1]
    src_sum, dst_sum, rel_sum = pl.pallas_call(
        functools.partial(bucket_kernel, width_block // chunk),
        out_shape=(
            jax.ShapeDtypeStruct(src_t.shape, jnp.float32),
            jax.ShapeDtypeStruct(dst_t.shape, jnp.float32),
            jax.ShapeDtypeStruct(rel_table.shape, jnp.float32),
        ),
        in_specs=[pl.BlockSpec(memory_space=pltpu.SMEM)] + [vmem] * 8,
        out_specs=[vmem] * 3,
        scratch_shapes=[
            pltpu.VMEM((width, rel_table.shape[0]), jnp.float32),
            pltpu.VMEM((dst_t.shape[1], chunk), jnp.float32),
        ],
        compiler_params=pltpu.CompilerParams(vmem_limit_bytes=56 * 2**20),
    )(
        count.reshape(1),
        s_all.reshape(steps, 1, chunk),
        t_all.reshape(steps, 1, chunk),
        r_all.reshape(steps, 1, chunk),
        negs.reshape(blocks, 1, negatives),
        src_t,
        dst_t.T,
        dst_t,
        rel_parts.astype(jnp.bfloat16).T,
    )
    return src_sum, dst_sum, rel_sum


def adagrad(table, state, grad):
    new_state = state + jnp.mean(grad * grad, axis=-1)
    return (table - LEARN_RATE * grad / jnp.sqrt(new_state)[..., None], new_state)


def body(
    n_src,
    n_dst,
    src_table,
    src_state,
    dst_table,
    dst_state,
    rel_table,
    rel_state,
    src_rows,
    dst_rows,
    rel_ids,
    counts,
    neg_rows,
):
    src_low = src_table.astype(jnp.bfloat16)[:, 0, :].T
    dst_low = dst_table.astype(jnp.bfloat16)[:, 0, :].T
    src_t, dst_t = gather(src_low, dst_low, n_src, n_dst)
    s_all = src_rows.reshape(-1)
    t_all = dst_rows.reshape(-1)
    r_all = rel_ids.reshape(-1)
    negs = neg_rows.reshape(neg_rows.shape[2], neg_rows.shape[3])
    count = counts.reshape(())
    src_sum, dst_sum, rel_sum = bucket_grads(
        src_t, dst_t, rel_table, s_all, t_all, r_all, negs, count
    )
    src_grad, dst_grad, rel_grad = reduce(src_sum, dst_sum, rel_sum, n_src, n_dst)
    new_src, new_src_state = adagrad(src_table, src_state, src_grad.T[:, None, :])
    new_dst, new_dst_state = adagrad(dst_table, dst_state, dst_grad.T[:, None, :])
    new_rel, new_rel_state = adagrad(rel_table, rel_state, rel_grad)
    return (new_src, new_src_state, new_dst, new_dst_state, new_rel, new_rel_state)


def solution(mesh):
    return jax.shard_map(
        functools.partial(body, mesh.shape["src"], mesh.shape["dst"]),
        mesh=mesh,
        in_specs=(
            P("dst", "src", None),
            P("dst", "src"),
            P("src", "dst", None),
            P("src", "dst"),
            P(),
            P(),
            P("src", "dst", None),
            P("src", "dst", None),
            P("src", "dst", None),
            P("src", "dst"),
            P("src", "dst", None, None),
        ),
        out_specs=(
            P("dst", "src", None),
            P("dst", "src"),
            P("src", "dst", None),
            P("src", "dst"),
            P(),
            P(),
        ),
        check_vma=False,
    )
```

```python
import functools

import jax
import jax.numpy as jnp
from jax import lax
from jax.experimental import pallas as pl
from jax.experimental.pallas import tpu as pltpu
from jax.sharding import PartitionSpec as P

LEARN_RATE = 0.1
CHUNK = 512
LOWEST = -1e30

NN = (((1,), (0,)), ((), ()))
NT = (((1,), (1,)), ((), ()))


def mm(a, b, dims=NN):
    return lax.dot_general(a, b, dims, preferred_element_type=jnp.float32)


def split(x):
    high = x.astype(jnp.bfloat16)
    return high, (x - high.astype(jnp.float32)).astype(jnp.bfloat16)


def one_hot(rows, idx):
    row = lax.broadcasted_iota(jnp.int32, (rows, idx.shape[1]), 0)
    return (row == idx).astype(jnp.float32).astype(jnp.bfloat16)


def bucket_kernel(
    per_block,
    count_ref,
    s_ref,
    t_ref,
    r_ref,
    neg_ref,
    src_t_ref,
    dst_ref,
    dst_t_ref,
    rel_parts_ref,
    src_sum_ref,
    dst_sum_ref,
    rel_sum_ref,
    src_grad_ref,
    dst_grad_ref,
    rel_grad_ref,
    times_ref,
):
    src_grad_ref[...] = jnp.zeros_like(src_grad_ref)
    dst_grad_ref[...] = jnp.zeros_like(dst_grad_ref)
    rel_grad_ref[...] = jnp.zeros_like(rel_grad_ref)
    count = count_ref[0]
    chunk = s_ref.shape[2]
    src_rows = src_t_ref.shape[1]
    dst_rows = dst_ref.shape[0]
    relations = rel_grad_ref.shape[1]

    @pl.loop(0, (count + chunk - 1) // chunk)
    def _(step):
        @pl.when(lax.rem(step, per_block) == 0)
        def _():
            neg = neg_ref[pl.ds(lax.div(step, per_block), 1), :]
            row = lax.broadcasted_iota(jnp.int32, (dst_rows, neg.shape[1]), 0)
            times = jnp.sum((row == neg).astype(jnp.float32), axis=1, keepdims=True)
            times_ref[...] = jnp.broadcast_to(times, times_ref.shape)

        slots = step * chunk + lax.broadcasted_iota(jnp.int32, (1, chunk), 1)
        valid = (slots < count).astype(jnp.float32)
        src_hot = one_hot(src_rows, s_ref[step])
        rel_hot = one_hot(relations, r_ref[step])
        src_emb = mm(src_t_ref[...], src_hot)
        rel_rows = mm(rel_parts_ref[...], jnp.concatenate([rel_hot] * 3, axis=0))
        query = (src_emb * rel_rows).astype(jnp.bfloat16)
        score = mm(dst_ref[...], query)
        is_pos = lax.broadcasted_iota(jnp.int32, score.shape, 0) == t_ref[step]
        times = times_ref[...]
        times = jnp.where(is_pos, times + 1.0, times)
        score = jnp.where(times > 0.0, score, LOWEST)
        top = jnp.max(score, axis=0, keepdims=True)
        terms = times * jnp.exp(score - top)
        weight = terms * (valid / jnp.sum(terms, axis=0, keepdims=True))
        weight = jnp.where(is_pos, weight - valid, weight)
        high, low = split(weight)
        dst_grad_ref[...] += mm(query, high, NT) + mm(query, low, NT)
        dquery = mm(dst_t_ref[...], high) + mm(dst_t_ref[...], low)
        high, low = split(dquery * rel_rows)
        src_grad_ref[...] += mm(high, src_hot, NT) + mm(low, src_hot, NT)
        high, low = split(dquery * src_emb)
        rel_grad_ref[...] += mm(high, rel_hot, NT) + mm(low, rel_hot, NT)

    src_sum_ref[...] = src_grad_ref[...].astype(jnp.bfloat16)
    dst_sum_ref[...] = dst_grad_ref[...].astype(jnp.bfloat16)
    row = lax.broadcasted_iota(jnp.int32, (relations, relations), 0)
    column = lax.broadcasted_iota(jnp.int32, (relations, relations), 1)
    rel_sum_ref[...] = lax.dot_general(
        (row == column).astype(jnp.float32),
        rel_grad_ref[...],
        NT,
        precision=lax.Precision.HIGHEST,
        preferred_element_type=jnp.float32,
    )


def exchange(axis, n, pairs, send_sem, recv_sem):
    me = lax.axis_index(axis)
    copies = []
    for k in range(1, n):
        peer = lax.rem(me + k, n)
        source, target = pairs(me, peer)
        copies.append(
            pltpu.make_async_remote_copy(
                src_ref=source,
                dst_ref=target,
                send_sem=send_sem.at[k - 1],
                recv_sem=recv_sem.at[k - 1],
                device_id={axis: peer},
                device_id_type=pl.DeviceIdType.MESH,
            )
        )
    for copy in copies:
        copy.start()
    return copies


def greet(sizes):
    barrier = pltpu.get_barrier_semaphore()
    for axis, n in sizes:
        me = lax.axis_index(axis)
        for k in range(1, n):
            pl.semaphore_signal(
                barrier,
                inc=1,
                device_id={axis: lax.rem(me + k, n)},
                device_id_type=pl.DeviceIdType.MESH,
            )
    pl.semaphore_wait(barrier, sum(n - 1 for _, n in sizes))


def lanes(index, rows):
    return pl.ds(pl.multiple_of(index * rows, rows), rows)


def gather_kernel(
    n_src,
    n_dst,
    src_wide,
    dst_wide,
    src_all,
    dst_all,
    src_ref,
    dst_ref,
    sends,
    recvs,
    send2,
    recv2,
):
    src_ref[...] = src_wide[...].astype(jnp.bfloat16)
    dst_ref[...] = dst_wide[...].astype(jnp.bfloat16)
    greet((("src", n_src), ("dst", n_dst)))
    rows = dst_ref.shape[1]
    mine = lanes(lax.axis_index("src"), rows)
    copies = exchange(
        "src", n_src, lambda me, peer: (dst_ref, dst_all.at[:, lanes(me, rows)]), sends, recvs
    )
    own_rows = src_ref.shape[1]
    own = lanes(lax.axis_index("dst"), own_rows)
    copies += exchange(
        "dst", n_dst, lambda me, peer: (src_ref, src_all.at[:, lanes(me, own_rows)]), send2, recv2
    )
    dst_all[:, mine] = dst_ref[...]
    src_all[:, own] = src_ref[...]
    for copy in copies:
        copy.wait()


def gather(src_part, dst_part, n_src, n_dst):
    vmem = pl.BlockSpec(memory_space=pltpu.VMEM)
    dma = pltpu.SemaphoreType.DMA
    width = src_part.shape[0]
    return pl.pallas_call(
        functools.partial(gather_kernel, n_src, n_dst),
        out_shape=(
            jax.ShapeDtypeStruct((width, src_part.shape[1] * n_dst), jnp.bfloat16),
            jax.ShapeDtypeStruct((width, dst_part.shape[1] * n_src), jnp.bfloat16),
        ),
        in_specs=[vmem] * 2,
        out_specs=[vmem] * 2,
        scratch_shapes=[
            pltpu.VMEM(src_part.shape, jnp.bfloat16),
            pltpu.VMEM(dst_part.shape, jnp.bfloat16),
            dma((n_src - 1,)),
            dma((n_src - 1,)),
            dma((n_dst - 1,)),
            dma((n_dst - 1,)),
        ],
        compiler_params=pltpu.CompilerParams(
            collective_id=0, has_side_effects=True, vmem_limit_bytes=32 * 2**20
        ),
    )(src_part, dst_part)


def total(slots, n):
    value = slots[0].astype(jnp.float32)
    for k in range(1, n):
        value = value + slots[k].astype(jnp.float32)
    return value


def reduce_kernel(
    n_src,
    n_dst,
    src_ref,
    dst_ref,
    rel_ref,
    src_out,
    dst_out,
    rel_out,
    src_slots,
    dst_slots,
    rel_slots,
    rel_slots2,
    part,
    *sems,
):
    greet((("src", n_src), ("dst", n_dst)))
    i, j = lax.axis_index("src"), lax.axis_index("dst")
    dst_rows, src_rows = dst_out.shape[1], src_out.shape[1]
    first = exchange("src", n_src, lambda me, peer: (rel_ref, rel_slots.at[me]), *sems[0:2])
    copies = exchange(
        "src",
        n_src,
        lambda me, peer: (dst_ref.at[:, lanes(peer, dst_rows)], dst_slots.at[me]),
        *sems[2:4],
    )
    src_copies = exchange(
        "dst",
        n_dst,
        lambda me, peer: (src_ref.at[:, lanes(peer, src_rows)], src_slots.at[me]),
        *sems[4:6],
    )
    rel_slots[i] = rel_ref[...]
    dst_slots[i] = dst_ref[:, lanes(i, dst_rows)]
    src_slots[j] = src_ref[:, lanes(j, src_rows)]
    for copy in first:
        copy.wait()
    part[...] = total(rel_slots, n_src)
    rel_slots2[j] = part[...]
    second = exchange("dst", n_dst, lambda me, peer: (part, rel_slots2.at[me]), *sems[6:8])
    for copy in src_copies:
        copy.wait()
    src_out[...] = total(src_slots, n_dst)
    for copy in second:
        copy.wait()
    rel_out[...] = total(rel_slots2, n_dst)
    for copy in copies:
        copy.wait()
    dst_out[...] = total(dst_slots, n_src)


def reduce(src_sum, dst_sum, rel_sum, n_src, n_dst):
    vmem = pl.BlockSpec(memory_space=pltpu.VMEM)
    dma = pltpu.SemaphoreType.DMA
    width = src_sum.shape[0]
    src_piece = (width, src_sum.shape[1] // n_dst)
    dst_piece = (width, dst_sum.shape[1] // n_src)
    counts = (n_src, n_src, n_dst, n_dst)
    return pl.pallas_call(
        functools.partial(reduce_kernel, n_src, n_dst),
        out_shape=tuple(
            jax.ShapeDtypeStruct(shape, jnp.float32)
            for shape in (src_piece, dst_piece, rel_sum.shape)
        ),
        in_specs=[vmem] * 3,
        out_specs=[vmem] * 3,
        scratch_shapes=[
            pltpu.VMEM((n_dst,) + src_piece, jnp.bfloat16),
            pltpu.VMEM((n_src,) + dst_piece, jnp.bfloat16),
            pltpu.VMEM((n_src,) + rel_sum.shape, jnp.float32),
            pltpu.VMEM((n_dst,) + rel_sum.shape, jnp.float32),
            pltpu.VMEM(rel_sum.shape, jnp.float32),
        ]
        + [dma((n - 1,)) for n in counts for _ in range(2)],
        compiler_params=pltpu.CompilerParams(
            collective_id=1, has_side_effects=True, vmem_limit_bytes=48 * 2**20
        ),
    )(src_sum, dst_sum, rel_sum)


def bucket_grads(src_t, dst_t, rel_table, s_all, t_all, r_all, negs, count):
    blocks = negs.shape[0]
    width_block = s_all.shape[0] // blocks
    chunk = CHUNK if width_block % CHUNK == 0 else width_block
    steps = s_all.shape[0] // chunk
    high = lax.reduce_precision(rel_table, 8, 7)
    middle = lax.reduce_precision(rel_table - high, 8, 7)
    rel_parts = jnp.concatenate([high, middle, rel_table - high - middle], axis=0)
    vmem = pl.BlockSpec(memory_space=pltpu.VMEM)
    width = rel_table.shape[1]
    src_sum, dst_sum, rel_sum = pl.pallas_call(
        functools.partial(bucket_kernel, width_block // chunk),
        out_shape=(
            jax.ShapeDtypeStruct(src_t.shape, jnp.bfloat16),
            jax.ShapeDtypeStruct(dst_t.shape, jnp.bfloat16),
            jax.ShapeDtypeStruct(rel_table.shape, jnp.float32),
        ),
        in_specs=[pl.BlockSpec(memory_space=pltpu.SMEM)] + [vmem] * 8,
        out_specs=[vmem] * 3,
        scratch_shapes=[
            pltpu.VMEM(src_t.shape, jnp.float32),
            pltpu.VMEM(dst_t.shape, jnp.float32),
            pltpu.VMEM((width, rel_table.shape[0]), jnp.float32),
            pltpu.VMEM((dst_t.shape[1], chunk), jnp.float32),
        ],
        compiler_params=pltpu.CompilerParams(vmem_limit_bytes=56 * 2**20),
    )(
        count.reshape(1),
        s_all.reshape(steps, 1, chunk),
        t_all.reshape(steps, 1, chunk),
        r_all.reshape(steps, 1, chunk),
        negs,
        src_t,
        dst_t.T,
        dst_t,
        rel_parts.astype(jnp.bfloat16).T,
    )
    return src_sum, dst_sum, rel_sum


def adagrad(table, state, grad):
    new_state = state + jnp.mean(grad * grad, axis=-1)
    return (table - LEARN_RATE * grad / jnp.sqrt(new_state)[..., None], new_state)


def body(
    n_src,
    n_dst,
    src_table,
    src_state,
    dst_table,
    dst_state,
    rel_table,
    rel_state,
    src_rows,
    dst_rows,
    rel_ids,
    counts,
    neg_rows,
):
    src_t, dst_t = gather(src_table[:, 0, :].T, dst_table[:, 0, :].T, n_src, n_dst)
    s_all = src_rows.reshape(-1)
    t_all = dst_rows.reshape(-1)
    r_all = rel_ids.reshape(-1)
    negs = neg_rows.reshape(neg_rows.shape[2], neg_rows.shape[3])
    count = counts.reshape(())
    src_sum, dst_sum, rel_sum = bucket_grads(
        src_t, dst_t, rel_table, s_all, t_all, r_all, negs, count
    )
    src_grad, dst_grad, rel_grad = reduce(src_sum, dst_sum, rel_sum, n_src, n_dst)
    new_src, new_src_state = adagrad(src_table, src_state, src_grad.T[:, None, :])
    new_dst, new_dst_state = adagrad(dst_table, dst_state, dst_grad.T[:, None, :])
    new_rel, new_rel_state = adagrad(rel_table, rel_state, rel_grad)
    return (new_src, new_src_state, new_dst, new_dst_state, new_rel, new_rel_state)


def solution(mesh):
    return jax.shard_map(
        functools.partial(body, mesh.shape["src"], mesh.shape["dst"]),
        mesh=mesh,
        in_specs=(
            P("dst", "src", None),
            P("dst", "src"),
            P("src", "dst", None),
            P("src", "dst"),
            P(),
            P(),
            P("src", "dst", None),
            P("src", "dst", None),
            P("src", "dst", None),
            P("src", "dst"),
            P("src", "dst", None, None),
        ),
        out_specs=(
            P("dst", "src", None),
            P("dst", "src"),
            P("src", "dst", None),
            P("src", "dst"),
            P(),
            P(),
        ),
        check_vma=False,
    )
```

```python
import functools

import jax
import jax.numpy as jnp
from jax import lax
from jax.experimental import pallas as pl
from jax.experimental.pallas import tpu as pltpu
from jax.sharding import PartitionSpec as P

LEARN_RATE = 0.1
CHUNK_ROWS = 2**20
LOWEST = -1e30

NN = (((1,), (0,)), ((), ()))
NT = (((1,), (1,)), ((), ()))


def mm(a, b, dims=NN):
    return lax.dot_general(a, b, dims, preferred_element_type=jnp.float32)


def split(x):
    high = x.astype(jnp.bfloat16)
    return high, (x - high.astype(jnp.float32)).astype(jnp.bfloat16)


def one_hot(rows, idx):
    row = lax.broadcasted_iota(jnp.int32, (rows, idx.shape[1]), 0)
    return (row == idx).astype(jnp.float32).astype(jnp.bfloat16)


def bucket_kernel(
    per_block,
    count_ref,
    s_ref,
    t_ref,
    r_ref,
    neg_ref,
    src_t_ref,
    dst_ref,
    dst_t_ref,
    rel_parts_ref,
    src_sum_ref,
    dst_sum_ref,
    rel_sum_ref,
    src_grad_ref,
    dst_grad_ref,
    rel_grad_ref,
    times_ref,
):
    src_grad_ref[...] = jnp.zeros_like(src_grad_ref)
    dst_grad_ref[...] = jnp.zeros_like(dst_grad_ref)
    rel_grad_ref[...] = jnp.zeros_like(rel_grad_ref)
    count = count_ref[0]
    chunk = s_ref.shape[2]
    src_rows = src_t_ref.shape[1]
    dst_rows = dst_ref.shape[0]
    relations = rel_grad_ref.shape[1]

    @pl.loop(0, (count + chunk - 1) // chunk)
    def _(step):
        @pl.when(lax.rem(step, per_block) == 0)
        def _():
            neg = neg_ref[pl.ds(lax.div(step, per_block), 1), :]
            row = lax.broadcasted_iota(jnp.int32, (dst_rows, neg.shape[1]), 0)
            times = jnp.sum((row == neg).astype(jnp.float32), axis=1, keepdims=True)
            times_ref[...] = jnp.broadcast_to(times, times_ref.shape)

        slots = step * chunk + lax.broadcasted_iota(jnp.int32, (1, chunk), 1)
        valid = (slots < count).astype(jnp.float32)
        src_hot = one_hot(src_rows, s_ref[step])
        rel_hot = one_hot(relations, r_ref[step])
        src_emb = mm(src_t_ref[...], src_hot)
        rel_rows = mm(rel_parts_ref[...], jnp.concatenate([rel_hot] * 3, axis=0))
        query = (src_emb * rel_rows).astype(jnp.bfloat16)
        score = mm(dst_ref[...], query)
        is_pos = lax.broadcasted_iota(jnp.int32, score.shape, 0) == t_ref[step]
        times = times_ref[...]
        times = jnp.where(is_pos, times + 1.0, times)
        score = jnp.where(times > 0.0, score, LOWEST)
        top = jnp.max(score, axis=0, keepdims=True)
        terms = times * jnp.exp(score - top)
        weight = terms * (valid / jnp.sum(terms, axis=0, keepdims=True))
        weight = jnp.where(is_pos, weight - valid, weight)
        high, low = split(weight)
        dst_grad_ref[...] += mm(query, high, NT) + mm(query, low, NT)
        dquery = mm(dst_t_ref[...], high) + mm(dst_t_ref[...], low)
        high, low = split(dquery * rel_rows)
        src_grad_ref[...] += mm(high, src_hot, NT) + mm(low, src_hot, NT)
        high, low = split(dquery * src_emb)
        rel_grad_ref[...] += mm(high, rel_hot, NT) + mm(low, rel_hot, NT)

    src_sum_ref[...] = src_grad_ref[...].astype(jnp.bfloat16)
    dst_sum_ref[...] = dst_grad_ref[...].astype(jnp.bfloat16)
    row = lax.broadcasted_iota(jnp.int32, (relations, relations), 0)
    column = lax.broadcasted_iota(jnp.int32, (relations, relations), 1)
    rel_sum_ref[...] = lax.dot_general(
        (row == column).astype(jnp.float32),
        rel_grad_ref[...],
        NT,
        precision=lax.Precision.HIGHEST,
        preferred_element_type=jnp.float32,
    )


def exchange(axis, n, pairs, send_sem, recv_sem):
    me = lax.axis_index(axis)
    copies = []
    for k in range(1, n):
        peer = lax.rem(me + k, n)
        source, target = pairs(me, peer)
        copies.append(
            pltpu.make_async_remote_copy(
                src_ref=source,
                dst_ref=target,
                send_sem=send_sem.at[k - 1],
                recv_sem=recv_sem.at[k - 1],
                device_id={axis: peer},
                device_id_type=pl.DeviceIdType.MESH,
            )
        )
    for copy in copies:
        copy.start()
    return copies


def greet(sizes):
    barrier = pltpu.get_barrier_semaphore()
    for axis, n in sizes:
        me = lax.axis_index(axis)
        for k in range(1, n):
            pl.semaphore_signal(
                barrier,
                inc=1,
                device_id={axis: lax.rem(me + k, n)},
                device_id_type=pl.DeviceIdType.MESH,
            )
    pl.semaphore_wait(barrier, sum(n - 1 for _, n in sizes))


def lanes(index, rows):
    return pl.ds(pl.multiple_of(index * rows, rows), rows)


def gather_kernel(
    n_src,
    n_dst,
    src_wide,
    dst_wide,
    src_all,
    dst_all,
    src_ref,
    dst_ref,
    sends,
    recvs,
    send2,
    recv2,
):
    src_ref[...] = src_wide[...].astype(jnp.bfloat16)
    dst_ref[...] = dst_wide[...].astype(jnp.bfloat16)
    greet((("src", n_src), ("dst", n_dst)))
    rows = dst_ref.shape[1]
    mine = lanes(lax.axis_index("src"), rows)
    copies = exchange(
        "src", n_src, lambda me, peer: (dst_ref, dst_all.at[:, lanes(me, rows)]), sends, recvs
    )
    own_rows = src_ref.shape[1]
    own = lanes(lax.axis_index("dst"), own_rows)
    copies += exchange(
        "dst", n_dst, lambda me, peer: (src_ref, src_all.at[:, lanes(me, own_rows)]), send2, recv2
    )
    dst_all[:, mine] = dst_ref[...]
    src_all[:, own] = src_ref[...]
    for copy in copies:
        copy.wait()


def gather(src_part, dst_part, n_src, n_dst):
    vmem = pl.BlockSpec(memory_space=pltpu.VMEM)
    dma = pltpu.SemaphoreType.DMA
    width = src_part.shape[0]
    return pl.pallas_call(
        functools.partial(gather_kernel, n_src, n_dst),
        out_shape=(
            jax.ShapeDtypeStruct((width, src_part.shape[1] * n_dst), jnp.bfloat16),
            jax.ShapeDtypeStruct((width, dst_part.shape[1] * n_src), jnp.bfloat16),
        ),
        in_specs=[vmem] * 2,
        out_specs=[vmem] * 2,
        scratch_shapes=[
            pltpu.VMEM(src_part.shape, jnp.bfloat16),
            pltpu.VMEM(dst_part.shape, jnp.bfloat16),
            dma((n_src - 1,)),
            dma((n_src - 1,)),
            dma((n_dst - 1,)),
            dma((n_dst - 1,)),
        ],
        compiler_params=pltpu.CompilerParams(
            collective_id=0, has_side_effects=True, vmem_limit_bytes=32 * 2**20
        ),
    )(src_part, dst_part)


def total(slots, n):
    value = slots[0].astype(jnp.float32)
    for k in range(1, n):
        value = value + slots[k].astype(jnp.float32)
    return value


def reduce_kernel(
    n_src,
    n_dst,
    src_ref,
    dst_ref,
    rel_ref,
    src_out,
    dst_out,
    rel_out,
    src_slots,
    dst_slots,
    rel_slots,
    rel_slots2,
    part,
    *sems,
):
    greet((("src", n_src), ("dst", n_dst)))
    i, j = lax.axis_index("src"), lax.axis_index("dst")
    dst_rows, src_rows = dst_out.shape[1], src_out.shape[1]
    first = exchange("src", n_src, lambda me, peer: (rel_ref, rel_slots.at[me]), *sems[0:2])
    copies = exchange(
        "src",
        n_src,
        lambda me, peer: (dst_ref.at[:, lanes(peer, dst_rows)], dst_slots.at[me]),
        *sems[2:4],
    )
    src_copies = exchange(
        "dst",
        n_dst,
        lambda me, peer: (src_ref.at[:, lanes(peer, src_rows)], src_slots.at[me]),
        *sems[4:6],
    )
    rel_slots[i] = rel_ref[...]
    dst_slots[i] = dst_ref[:, lanes(i, dst_rows)]
    src_slots[j] = src_ref[:, lanes(j, src_rows)]
    for copy in first:
        copy.wait()
    part[...] = total(rel_slots, n_src)
    rel_slots2[j] = part[...]
    second = exchange("dst", n_dst, lambda me, peer: (part, rel_slots2.at[me]), *sems[6:8])
    for copy in src_copies:
        copy.wait()
    src_out[...] = total(src_slots, n_dst)
    for copy in second:
        copy.wait()
    rel_out[...] = total(rel_slots2, n_dst)
    for copy in copies:
        copy.wait()
    dst_out[...] = total(dst_slots, n_src)


def reduce(src_sum, dst_sum, rel_sum, n_src, n_dst):
    vmem = pl.BlockSpec(memory_space=pltpu.VMEM)
    dma = pltpu.SemaphoreType.DMA
    width = src_sum.shape[0]
    src_piece = (width, src_sum.shape[1] // n_dst)
    dst_piece = (width, dst_sum.shape[1] // n_src)
    counts = (n_src, n_src, n_dst, n_dst)
    return pl.pallas_call(
        functools.partial(reduce_kernel, n_src, n_dst),
        out_shape=tuple(
            jax.ShapeDtypeStruct(shape, jnp.float32)
            for shape in (src_piece, dst_piece, rel_sum.shape)
        ),
        in_specs=[vmem] * 3,
        out_specs=[vmem] * 3,
        scratch_shapes=[
            pltpu.VMEM((n_dst,) + src_piece, jnp.bfloat16),
            pltpu.VMEM((n_src,) + dst_piece, jnp.bfloat16),
            pltpu.VMEM((n_src,) + rel_sum.shape, jnp.float32),
            pltpu.VMEM((n_dst,) + rel_sum.shape, jnp.float32),
            pltpu.VMEM(rel_sum.shape, jnp.float32),
        ]
        + [dma((n - 1,)) for n in counts for _ in range(2)],
        compiler_params=pltpu.CompilerParams(
            collective_id=1, has_side_effects=True, vmem_limit_bytes=48 * 2**20
        ),
    )(src_sum, dst_sum, rel_sum)


def bucket_grads(src_t, dst_t, rel_table, s_all, t_all, r_all, negs, count):
    blocks = negs.shape[0]
    width_block = s_all.shape[0] // blocks
    chunk = min(width_block, max(128, CHUNK_ROWS // dst_t.shape[1]))
    chunk = chunk if width_block % chunk == 0 else width_block
    steps = s_all.shape[0] // chunk
    high = lax.reduce_precision(rel_table, 8, 7)
    middle = lax.reduce_precision(rel_table - high, 8, 7)
    rel_parts = jnp.concatenate([high, middle, rel_table - high - middle], axis=0)
    vmem = pl.BlockSpec(memory_space=pltpu.VMEM)
    width = rel_table.shape[1]
    src_sum, dst_sum, rel_sum = pl.pallas_call(
        functools.partial(bucket_kernel, width_block // chunk),
        out_shape=(
            jax.ShapeDtypeStruct(src_t.shape, jnp.bfloat16),
            jax.ShapeDtypeStruct(dst_t.shape, jnp.bfloat16),
            jax.ShapeDtypeStruct(rel_table.shape, jnp.float32),
        ),
        in_specs=[pl.BlockSpec(memory_space=pltpu.SMEM)] + [vmem] * 8,
        out_specs=[vmem] * 3,
        scratch_shapes=[
            pltpu.VMEM(src_t.shape, jnp.float32),
            pltpu.VMEM(dst_t.shape, jnp.float32),
            pltpu.VMEM((width, rel_table.shape[0]), jnp.float32),
            pltpu.VMEM((dst_t.shape[1], chunk), jnp.float32),
        ],
        compiler_params=pltpu.CompilerParams(vmem_limit_bytes=56 * 2**20),
    )(
        count.reshape(1),
        s_all.reshape(steps, 1, chunk),
        t_all.reshape(steps, 1, chunk),
        r_all.reshape(steps, 1, chunk),
        negs,
        src_t,
        dst_t.T,
        dst_t,
        rel_parts.astype(jnp.bfloat16).T,
    )
    return src_sum, dst_sum, rel_sum


def adagrad(table, state, grad):
    new_state = state + jnp.mean(grad * grad, axis=-1)
    return (table - LEARN_RATE * grad / jnp.sqrt(new_state)[..., None], new_state)


def body(
    n_src,
    n_dst,
    src_table,
    src_state,
    dst_table,
    dst_state,
    rel_table,
    rel_state,
    src_rows,
    dst_rows,
    rel_ids,
    counts,
    neg_rows,
):
    src_t, dst_t = gather(src_table[:, 0, :].T, dst_table[:, 0, :].T, n_src, n_dst)
    s_all = src_rows.reshape(-1)
    t_all = dst_rows.reshape(-1)
    r_all = rel_ids.reshape(-1)
    negs = neg_rows.reshape(neg_rows.shape[2], neg_rows.shape[3])
    count = counts.reshape(())
    src_sum, dst_sum, rel_sum = bucket_grads(
        src_t, dst_t, rel_table, s_all, t_all, r_all, negs, count
    )
    src_grad, dst_grad, rel_grad = reduce(src_sum, dst_sum, rel_sum, n_src, n_dst)
    new_src, new_src_state = adagrad(src_table, src_state, src_grad.T[:, None, :])
    new_dst, new_dst_state = adagrad(dst_table, dst_state, dst_grad.T[:, None, :])
    new_rel, new_rel_state = adagrad(rel_table, rel_state, rel_grad)
    return (new_src, new_src_state, new_dst, new_dst_state, new_rel, new_rel_state)


def solution(mesh):
    return jax.shard_map(
        functools.partial(body, mesh.shape["src"], mesh.shape["dst"]),
        mesh=mesh,
        in_specs=(
            P("dst", "src", None),
            P("dst", "src"),
            P("src", "dst", None),
            P("src", "dst"),
            P(),
            P(),
            P("src", "dst", None),
            P("src", "dst", None),
            P("src", "dst", None),
            P("src", "dst"),
            P("src", "dst", None, None),
        ),
        out_specs=(
            P("dst", "src", None),
            P("dst", "src"),
            P("src", "dst", None),
            P("src", "dst"),
            P(),
            P(),
        ),
        check_vma=False,
    )
```
